32 devices in a mesh: dp: 2 (over x), mp: 16 (over z, y, core).
Axes of the slice: x: 2, y: 2, z: 4, core: 2. Of those that a mesh axis runs over, the one named last changes fastest.
Arguments:
- inputs: bfloat16 [1024, 4608], P(('dp', 'mp')), may hold values from -6 to 6
- lengths: int32 [2], P('dp'), may hold values from 1 to 512, as said below
- gain_in: float32 [4608], replicated, may hold values from 0.1 to 1.9
- query_weight: float32 [4608, 4096], P('dp', 'mp'), may hold values from -0.11785113 to 0.11785113
- key_weight: float32 [4608, 2048], P('dp', 'mp'), may hold values from -0.11785113 to 0.11785113
- value_weight: float32 [4608, 2048], P('dp', 'mp'), may hold values from -0.09375 to 0.09375
- output_weight: bfloat16 [4096, 4608], P('mp'), may hold values from -0.09375 to 0.09375
- gain_post: float32 [4608], replicated, may hold values from 0.1 to 1.9
- gain_pre: float32 [4608], replicated, may hold values from 0.1 to 1.9
- gate_weight: float32 [4608, 20480], P('dp', 'mp'), may hold values from -0.09375 to 0.09375
- up_weight: float32 [4608, 20480], P('dp', 'mp'), may hold values from -0.09375 to 0.09375
Outputs:
- residual: bfloat16 [1024, 4608], P(('dp', 'mp'))
- hidden: bfloat16 [1024, 20480], P('dp', 'mp')
- keys_out: bfloat16 [1024, 2048], P('dp', 'mp')
- values_out: bfloat16 [1024, 2048], P('dp', 'mp')
The draws below stay inside these ranges and needn't reach their ends.
Inputs may be any that keep to these rules, and one draw needn't show every extreme that they name: Half of the 2 prompts have lengths under 512 // 16, the others at least 448; at least one prompt fills its slot.
All inputs are finite; a program needn't handle non-finite values.
Results may differ from the reference program's by a relative error of at most 0.03.
Values may be sent and summed in bfloat16 or wider, within the bound.
A program may use at most 128 MiB of HBM per device.

```python
import math
import jax
import jax.numpy as jnp
from jax import lax

D = 4608
HQ = 32
KVH = 16
HD = 128
FFW = 20480
SLOT = 512
PROMPTS = 2
TOKENS = 1024
N_MP = 16


def draw_lengths(key, part):
    key_short, key_long, key_order = jax.random.split(key, 3)
    count = PROMPTS
    half_count = count // 2
    short_len = jax.random.randint(key_short, (count,), 1, SLOT // 16)
    long_len = jax.random.randint(key_long, (count,), SLOT - SLOT // 8, SLOT + 1)
    slots_idx = jnp.arange(count, dtype=jnp.int32)
    long_len = jnp.where(slots_idx == half_count, SLOT, long_len)
    chosen = jnp.where(slots_idx < half_count, short_len, long_len).astype(jnp.int32)
    order = jax.random.permutation(key_order, count)
    return chosen[order]


def shared_parts(key):
    common_key = jax.random.fold_in(key, 7711)
    key_dir, key_head = jax.random.split(common_key, 2)
    direction = jax.random.rademacher(key_dir, (D,), dtype=jnp.float32)
    head_dirs = jnp.clip(jax.random.normal(key_head, (KVH, HD), jnp.float32), -3.0, 3.0)
    return (direction, head_dirs)


def projection_draw(key, seed_salt, head_count, repeat_count):
    direction, head_dirs = shared_parts(key)
    key_base, key_strength = jax.random.split(jax.random.fold_in(key, seed_salt), 2)
    columns = head_count * HD
    base_part = jnp.clip(jax.random.normal(key_base, (D, columns), jnp.float32), -4.0, 4.0)
    strength = jnp.exp(jax.random.uniform(key_strength, (head_count,), jnp.float32, math.log(0.5), math.log(2.2)))
    per_head = jnp.repeat(head_dirs, repeat_count, axis=0) * strength[:, None]
    weights_all = (base_part + direction[:, None] * per_head.reshape(columns)[None, :]) * (1.0 / math.sqrt(D))
    limit_value = 8.0 / math.sqrt(D)
    return jnp.clip(weights_all, -limit_value, limit_value)


def draw_query_weight(key, part):
    return projection_draw(key, 31, HQ, HQ // KVH)


def draw_key_weight(key, part):
    return projection_draw(key, 37, KVH, 1)


def shard_levels(own_key, shape, pieces, low, top_value):
    loudness, own = 1.0, jax.random.fold_in(own_key, 6)
    for position, blocks in pieces:
        steps = jnp.exp(jax.random.uniform(jax.random.fold_in(own, position), (blocks,), jnp.float32, low / len(pieces), top_value / len(pieces)))
        loudness = loudness * jnp.repeat(steps, shape[position] // blocks).reshape([-1 if axis == position else 1 for axis in range(len(shape))])
    return loudness


def centred(stream_key, dims, scale, most, cuts=(), kind=jnp.bfloat16):
    drawn = jax.random.normal(stream_key, dims, jnp.float32) * scale
    if len(cuts) > 0:
        drawn = shard_levels(stream_key, dims, cuts, -0.22, 0.18) * drawn
    return jnp.clip(drawn, min=-most, max=most).astype(kind)


def setup_inputs(seed: int = 0) -> dict:
    streams_of = jax.random.split(jax.random.key(seed), 12)
    inputs = centred(streams_of[0], (TOKENS, D), 1.0, 6.0, ((0, 32),))
    lengths = draw_lengths(jax.random.fold_in(streams_of[11], 71), 0)
    gain_in = jnp.clip(1.0 + 0.18 * jax.random.normal(streams_of[2], (D,), jnp.float32), 0.1, 1.9)
    query_weight = draw_query_weight(jax.random.fold_in(streams_of[11], 71), 0)
    key_weight = draw_key_weight(jax.random.fold_in(streams_of[11], 71), 0)
    value_weight = centred(streams_of[5], (D, KVH * HD), D ** -0.5, 0.09375, ((0, 2), (1, 16)), jnp.float32)
    output_weight = centred(streams_of[6], (HQ * HD, D), (HQ * HD) ** -0.5, 0.09375, ((0, 16),))
    gain_post = jnp.clip(1.0 + 0.18 * jax.random.normal(streams_of[7], (D,), jnp.float32), 0.1, 1.9)
    gain_pre = jnp.clip(1.0 + 0.18 * jax.random.normal(streams_of[8], (D,), jnp.float32), 0.1, 1.9)
    gate_weight = centred(streams_of[9], (D, FFW), D ** -0.5, 0.09375, ((0, 2), (1, 16)), jnp.float32)
    up_weight = centred(streams_of[10], (D, FFW), D ** -0.5, 0.09375, ((0, 2), (1, 16)), jnp.float32)
    return {"inputs": inputs, "lengths": lengths, "gain_in": gain_in, "query_weight": query_weight, "key_weight": key_weight, "value_weight": value_weight, "output_weight": output_weight, "gain_post": gain_post, "gain_pre": gain_pre, "gate_weight": gate_weight, "up_weight": up_weight}


query_scale = 1.0 / 12.0
soft_cap = 50.0

def rms_norm(values, gain):
    mean_sq = lax.optimization_barrier(jnp.mean(values * values, axis=-1, keepdims=True))
    return values * lax.rsqrt(mean_sq + 1e-06) * gain

def rotate_pairs(values, positions):
    half_size = values.shape[-1] // 2
    freqs = jnp.exp(jnp.arange(half_size, dtype=jnp.float32) * (-2.0 * math.log(10000.0) / values.shape[-1]))
    angles = positions.astype(jnp.float32)[:, None] * freqs[None, :]
    cosine = jnp.cos(angles)[:, None, :]
    sine = jnp.sin(angles)[:, None, :]
    first = values[..., :half_size]
    second = values[..., half_size:]
    return jnp.concatenate([first * cosine - second * sine, second * cosine + first * sine], axis=-1)

def reference(inputs, lengths, gain_in, query_weight, key_weight, value_weight, output_weight, gain_post, gain_pre, gate_weight, up_weight):
    tokens = inputs.shape[0]
    prompts = lengths.shape[0]
    slot = tokens // prompts
    positions = jnp.arange(tokens, dtype=jnp.int32) % slot
    row_len = jnp.repeat(lengths, slot, total_repeat_length=tokens)
    live = positions < row_len
    normed = rms_norm(inputs.astype(jnp.float32), gain_in).astype(jnp.bfloat16)
    raw_q = jnp.dot(normed, query_weight.astype(jnp.bfloat16), preferred_element_type=jnp.float32)
    raw_k = jnp.dot(normed, key_weight.astype(jnp.bfloat16), preferred_element_type=jnp.float32)
    raw_v = jnp.dot(normed, value_weight.astype(jnp.bfloat16), preferred_element_type=jnp.float32)
    queries = rotate_pairs(raw_q.reshape(tokens, HQ, HD), positions).astype(jnp.bfloat16)
    keys_rot = rotate_pairs(raw_k.reshape(tokens, KVH, HD), positions)
    keys_rot = jnp.where(live[:, None, None], keys_rot, jnp.float32(0.0)).astype(jnp.bfloat16)
    values_all = jnp.where(live[:, None], raw_v, jnp.float32(0.0)).astype(jnp.bfloat16).reshape(tokens, KVH, HD)

    def attend(operands):
        query_block, key_block, value_block, length = operands
        key_rep = jnp.repeat(key_block, HQ // KVH, axis=1).astype(jnp.float32)
        value_rep = jnp.repeat(value_block, HQ // KVH, axis=1).astype(jnp.float32)
        scores = jnp.einsum('qhd,khd->hqk', query_block.astype(jnp.float32), key_rep) * query_scale
        capped = soft_cap * jnp.tanh(scores / soft_cap)
        slot_pos = jnp.arange(slot, dtype=jnp.int32)
        allowed = (slot_pos[None, :] <= slot_pos[:, None]) & (slot_pos[None, :] < length)
        weights_exp = jnp.where(allowed[None], jnp.exp(capped), jnp.float32(0.0))
        probs = (weights_exp / lax.optimization_barrier(jnp.sum(weights_exp, axis=-1, keepdims=True))).astype(jnp.bfloat16)
        mixed = jnp.einsum('hqk,khd->qhd', probs.astype(jnp.float32), value_rep)
        mixed = jnp.where((slot_pos < length)[:, None, None], mixed, jnp.float32(0.0))
        return mixed.astype(jnp.bfloat16)
    attended = lax.map(attend, (queries.reshape(prompts, slot, HQ, HD), keys_rot.reshape(prompts, slot, KVH, HD), values_all.reshape(prompts, slot, KVH, HD), lengths))
    attended = attended.reshape(tokens, HQ * HD)
    group_width = HQ * HD // N_MP
    attn = jnp.zeros((tokens, inputs.shape[1]), jnp.float32)
    for group in range(N_MP):
        part_term = jnp.dot(attended[:, group * group_width:(group + 1) * group_width], output_weight[group * group_width:(group + 1) * group_width], preferred_element_type=jnp.float32)
        attn = attn + part_term.astype(jnp.bfloat16).astype(jnp.float32)
    residual = (inputs.astype(jnp.float32) + rms_norm(attn, gain_post)).astype(jnp.bfloat16)
    pre_ffn = rms_norm(residual.astype(jnp.float32), gain_pre).astype(jnp.bfloat16)
    gate = jnp.dot(pre_ffn, gate_weight.astype(jnp.bfloat16), preferred_element_type=jnp.float32)
    up_part = jnp.dot(pre_ffn, up_weight.astype(jnp.bfloat16), preferred_element_type=jnp.float32)
    hidden = (jax.nn.gelu(gate, approximate=True) * up_part).astype(jnp.bfloat16)
    return (residual, hidden, keys_rot.reshape(tokens, KVH * HD), values_all.reshape(tokens, KVH * HD))
```

```python
import math

import jax
import jax.numpy as jnp
from jax import lax
from jax.sharding import PartitionSpec as P

KVH = 16


query_scale = 1.0 / 12.0
soft_cap = 50.0


def swapped(value, axis, stride):
    mask = 2**stride
    pairs = [(source, source ^ mask) for source in range(lax.axis_size(axis))]
    return lax.ppermute(value, axis, pairs)


def rms_norm(values, gain):
    mean_sq = jnp.mean(values * values, axis=-1, keepdims=True)
    return values * lax.rsqrt(mean_sq + 1e-06) * gain


def rotate_pairs(values, positions):
    half_size = values.shape[-1] // 2
    freqs = jnp.exp(
        jnp.arange(half_size, dtype=jnp.float32) * (-2.0 * math.log(10000.0) / values.shape[-1])
    )
    angles = positions.astype(jnp.float32)[:, None] * freqs[None, :]
    cosine = jnp.cos(angles)[:, None, :]
    sine = jnp.sin(angles)[:, None, :]
    first = values[..., :half_size]
    second = values[..., half_size:]
    return jnp.concatenate(
        [first * cosine - second * sine, second * cosine + first * sine], axis=-1
    )


def join_halves(own_half, other_half, odd_flag):
    lower_first = jnp.concatenate([own_half, other_half], axis=1)
    upper_first = jnp.concatenate([other_half, own_half], axis=1)
    return jnp.where(odd_flag, upper_first, lower_first)


def head_block(query_rows, key_rows, value_rows, key_count, length):
    scores = (
        jnp.einsum("qhd,kd->hqk", query_rows, key_rows, preferred_element_type=jnp.float32)
        * query_scale
    )
    capped = soft_cap * jnp.tanh(scores / soft_cap)
    query_pos = jnp.arange(query_rows.shape[0], dtype=jnp.int32)
    key_pos = jnp.arange(key_count, dtype=jnp.int32)
    allowed = (key_pos[None, :] <= query_pos[:, None]) & (key_pos[None, :] < length)
    weights_exp = jnp.where(allowed[None], jnp.exp(capped), jnp.float32(0.0))
    probs = (weights_exp / jnp.sum(weights_exp, axis=-1, keepdims=True)).astype(jnp.bfloat16)
    return jnp.einsum("hqk,kd->qhd", probs, value_rows, preferred_element_type=jnp.float32)


def on_device(
    inputs,
    lengths,
    gain_in,
    query_weight,
    key_weight,
    value_weight,
    output_weight,
    gain_post,
    gain_pre,
    gate_weight,
    up_weight,
):
    mp_count = lax.axis_size("mp")
    mp_index = lax.axis_index("mp")
    odd_flag = mp_index % 2 == 1
    paired = mp_count > KVH
    gate_bf = gate_weight.astype(jnp.bfloat16)
    up_bf = up_weight.astype(jnp.bfloat16)
    normed_local = rms_norm(inputs.astype(jnp.float32), gain_in).astype(jnp.bfloat16)
    normed = lax.all_gather(normed_local, "mp", axis=0, tiled=True)
    group_tokens = normed.shape[0]
    prompts = lengths.shape[0]
    slot = group_tokens // prompts
    query_bf = query_weight.astype(jnp.bfloat16)
    key_bf = key_weight.astype(jnp.bfloat16)
    value_bf = value_weight.astype(jnp.bfloat16)
    own_width = key_weight.shape[1]
    if paired:
        other_key, other_value = swapped((key_bf, value_bf), "mp", 0)
        key_bf = join_halves(key_bf, other_key, odd_flag)
        value_bf = join_halves(value_bf, other_value, odd_flag)
    pieces = (
        lax.all_gather(query_bf, "dp", axis=0, tiled=True),
        lax.all_gather(key_bf, "dp", axis=0, tiled=True),
        lax.all_gather(value_bf, "dp", axis=0, tiled=True),
    )
    columns = normed
    raw_q, raw_k, raw_v = tuple(
        (jnp.dot(columns, piece, preferred_element_type=jnp.float32) for piece in pieces)
    )
    head_size = raw_k.shape[1]
    local_heads = raw_q.shape[1] // head_size
    positions = jnp.arange(group_tokens, dtype=jnp.int32) % slot
    row_len = jnp.repeat(lengths, slot, total_repeat_length=group_tokens)
    live = positions < row_len
    queries = rotate_pairs(raw_q.reshape(group_tokens, local_heads, head_size), positions).astype(
        jnp.bfloat16
    )
    keys_rot = rotate_pairs(raw_k.reshape(group_tokens, 1, head_size), positions).reshape(
        group_tokens, head_size
    )
    keys_rot = jnp.where(live[:, None], keys_rot, jnp.float32(0.0)).astype(jnp.bfloat16)
    values_all = jnp.where(live[:, None], raw_v, jnp.float32(0.0)).astype(jnp.bfloat16)
    key_rows = keys_rot[0:slot]
    value_rows = values_all[0:slot]
    length = lengths[0]
    mixed = head_block(queries, key_rows, value_rows, slot, length)
    slot_pos = jnp.arange(slot, dtype=jnp.int32)
    mixed = jnp.where((slot_pos < length)[:, None, None], mixed, jnp.float32(0.0))
    attended_list = mixed.astype(jnp.bfloat16).reshape(slot, local_heads * head_size)
    attn_rows = lax.psum_scatter(
        jnp.dot(attended_list, output_weight, preferred_element_type=jnp.float32).astype(
            jnp.bfloat16
        ),
        "mp",
        scatter_dimension=0,
        tiled=True,
    ).astype(jnp.float32)
    residual = (inputs.astype(jnp.float32) + rms_norm(attn_rows, gain_post)).astype(jnp.bfloat16)
    pre_local = rms_norm(residual.astype(jnp.float32), gain_pre).astype(jnp.bfloat16)
    pre_ffn = lax.all_gather(pre_local, "mp", axis=0, tiled=True)
    pieces = (
        lax.all_gather(gate_bf, "dp", axis=0, tiled=True),
        lax.all_gather(up_bf, "dp", axis=0, tiled=True),
    )
    columns = pre_ffn
    gate = jnp.dot(columns, pieces[0], preferred_element_type=jnp.float32)
    up_part = jnp.dot(columns, pieces[1], preferred_element_type=jnp.float32)
    hidden = (jax.nn.gelu(gate, approximate=True) * up_part).astype(jnp.bfloat16)
    if paired:
        offset = mp_index % 2 * own_width
        keys_out = lax.dynamic_slice_in_dim(keys_rot, offset, own_width, 1)
        values_out = lax.dynamic_slice_in_dim(values_all, offset, own_width, 1)
    else:
        keys_out = keys_rot
        values_out = values_all
    return (residual, hidden, keys_out, values_out)


def swap_dp(value):
    return lax.ppermute(value, "dp", [(0, 1), (1, 0)])


def gather_mp(block):
    return lax.all_gather(block, "mp", axis=0, tiled=True)


def scatter_mp(partial):
    return lax.psum_scatter(partial, "mp", scatter_dimension=0, tiled=True)


def split_rows(block):
    half = block.shape[1] // 2
    index = lax.axis_index("dp")
    own = lax.dynamic_slice_in_dim(block, index * half, half, 1)
    other = lax.dynamic_slice_in_dim(block, (1 - index) * half, half, 1)
    return own, other


def exchange_gather(block):
    own, other = split_rows(block)
    arrived = swap_dp(other)
    own, arrived = lax.optimization_barrier((own, arrived))
    partner_tokens = gather_mp(arrived)
    own_tokens = gather_mp(own)
    return own_tokens, partner_tokens


def on_device_pair(
    inputs,
    lengths,
    gain_in,
    query_weight,
    key_weight,
    value_weight,
    output_weight,
    gain_post,
    gain_pre,
    gate_weight,
    up_weight,
):
    bf16 = jnp.bfloat16
    slot = inputs.shape[0] * lax.axis_size("mp")
    length = lengths[0]
    normed_local = rms_norm(inputs.astype(jnp.float32), gain_in).astype(bf16)
    own_tokens, partner_tokens = exchange_gather(normed_local)
    qkv_weight = jnp.concatenate([query_weight, key_weight, value_weight], axis=1).astype(bf16)
    head_size = key_weight.shape[1]
    local_heads = query_weight.shape[1] // head_size
    partner_part = jnp.dot(partner_tokens, qkv_weight, preferred_element_type=jnp.float32)
    arrived = swap_dp(partner_part.astype(bf16))
    raw = jnp.dot(own_tokens, qkv_weight, preferred_element_type=jnp.float32)
    raw = raw + arrived.astype(jnp.float32)
    q_cols = local_heads * head_size
    raw_q, raw_k, raw_v = (
        raw[:, :q_cols],
        raw[:, q_cols : q_cols + head_size],
        raw[:, q_cols + head_size :],
    )
    positions = jnp.arange(slot, dtype=jnp.int32)
    live = positions < length
    queries = rotate_pairs(raw_q.reshape(slot, local_heads, head_size), positions).astype(bf16)
    keys_rot = rotate_pairs(raw_k.reshape(slot, 1, head_size), positions).reshape(slot, head_size)
    keys_rot = jnp.where(live[:, None], keys_rot, jnp.float32(0.0)).astype(bf16)
    values_all = jnp.where(live[:, None], raw_v, jnp.float32(0.0)).astype(bf16)
    mixed = head_block(queries, keys_rot, values_all, slot, length)
    mixed = jnp.where(live[:, None, None], mixed, jnp.float32(0.0))
    attended = mixed.astype(bf16).reshape(slot, local_heads * head_size)
    attn_rows = scatter_mp(
        jnp.dot(attended, output_weight, preferred_element_type=jnp.float32).astype(bf16)
    ).astype(jnp.float32)
    residual = (inputs.astype(jnp.float32) + rms_norm(attn_rows, gain_post)).astype(bf16)
    pre_local = rms_norm(residual.astype(jnp.float32), gain_pre).astype(bf16)
    own_tokens, partner_tokens = exchange_gather(pre_local)
    columns = gate_weight.shape[1]
    width = 256
    weights = []
    sent = []
    for start in range(0, columns, width):
        pair = tuple(
            weight[:, start : start + width].astype(bf16) for weight in (gate_weight, up_weight)
        )
        weights.append(pair)
        sent.append(
            tuple(
                swap_dp(
                    jnp.dot(partner_tokens, piece, preferred_element_type=jnp.float32).astype(bf16)
                )
                for piece in pair
            )
        )
    hidden = []
    for pair, arrived in zip(weights, sent):
        gate, up_part = tuple(
            jnp.dot(own_tokens, piece, preferred_element_type=jnp.float32)
            + other.astype(jnp.float32)
            for piece, other in zip(pair, arrived)
        )
        hidden.append((jax.nn.gelu(gate, approximate=True) * up_part).astype(bf16))
    return (residual, jnp.concatenate(hidden, axis=1), keys_rot, values_all)


def solution(mesh):
    pair_form = mesh.shape["dp"] == 2 and mesh.shape["mp"] <= KVH
    in_specs = (
        P(("dp", "mp"), None),
        P("dp"),
        P(),
        P("dp", "mp"),
        P("dp", "mp"),
        P("dp", "mp"),
        P("mp", None),
        P(),
        P(),
        P("dp", "mp"),
        P("dp", "mp"),
    )
    out_specs = (P(("dp", "mp"), None), P("dp", "mp"), P("dp", "mp"), P("dp", "mp"))
    return jax.shard_map(
        on_device_pair if pair_form else on_device, mesh=mesh, in_specs=in_specs, out_specs=out_specs, check_vma=False
    )
```

```python
import functools
import math

import jax
import jax.numpy as jnp
from jax import lax
from jax.experimental import pallas as pl
from jax.experimental.pallas import tpu as pltpu
from jax.sharding import PartitionSpec as P

KVH = 16


query_scale = 1.0 / 12.0
soft_cap = 50.0


def swapped(value, axis, stride):
    mask = 2**stride
    pairs = [(source, source ^ mask) for source in range(lax.axis_size(axis))]
    return lax.ppermute(value, axis, pairs)


def rms_norm(values, gain):
    mean_sq = jnp.mean(values * values, axis=-1, keepdims=True)
    return values * lax.rsqrt(mean_sq + 1e-06) * gain


def rotate_pairs(values, positions):
    half_size = values.shape[-1] // 2
    freqs = jnp.exp(
        jnp.arange(half_size, dtype=jnp.float32) * (-2.0 * math.log(10000.0) / values.shape[-1])
    )
    angles = positions.astype(jnp.float32)[:, None] * freqs[None, :]
    cosine = jnp.cos(angles)[:, None, :]
    sine = jnp.sin(angles)[:, None, :]
    first = values[..., :half_size]
    second = values[..., half_size:]
    return jnp.concatenate(
        [first * cosine - second * sine, second * cosine + first * sine], axis=-1
    )


def join_halves(own_half, other_half, odd_flag):
    lower_first = jnp.concatenate([own_half, other_half], axis=1)
    upper_first = jnp.concatenate([other_half, own_half], axis=1)
    return jnp.where(odd_flag, upper_first, lower_first)


def head_block(query_rows, key_rows, value_rows, key_count, length):
    scores = (
        jnp.einsum("qhd,kd->hqk", query_rows, key_rows, preferred_element_type=jnp.float32)
        * query_scale
    )
    capped = soft_cap * jnp.tanh(scores / soft_cap)
    query_pos = jnp.arange(query_rows.shape[0], dtype=jnp.int32)
    key_pos = jnp.arange(key_count, dtype=jnp.int32)
    allowed = (key_pos[None, :] <= query_pos[:, None]) & (key_pos[None, :] < length)
    weights_exp = jnp.where(allowed[None], jnp.exp(capped), jnp.float32(0.0))
    probs = (weights_exp / jnp.sum(weights_exp, axis=-1, keepdims=True)).astype(jnp.bfloat16)
    return jnp.einsum("hqk,kd->qhd", probs, value_rows, preferred_element_type=jnp.float32)


def on_device(
    inputs,
    lengths,
    gain_in,
    query_weight,
    key_weight,
    value_weight,
    output_weight,
    gain_post,
    gain_pre,
    gate_weight,
    up_weight,
):
    mp_count = lax.axis_size("mp")
    mp_index = lax.axis_index("mp")
    odd_flag = mp_index % 2 == 1
    paired = mp_count > KVH
    gate_bf = gate_weight.astype(jnp.bfloat16)
    up_bf = up_weight.astype(jnp.bfloat16)
    normed_local = rms_norm(inputs.astype(jnp.float32), gain_in).astype(jnp.bfloat16)
    normed = lax.all_gather(normed_local, "mp", axis=0, tiled=True)
    group_tokens = normed.shape[0]
    prompts = lengths.shape[0]
    slot = group_tokens // prompts
    query_bf = query_weight.astype(jnp.bfloat16)
    key_bf = key_weight.astype(jnp.bfloat16)
    value_bf = value_weight.astype(jnp.bfloat16)
    own_width = key_weight.shape[1]
    if paired:
        other_key, other_value = swapped((key_bf, value_bf), "mp", 0)
        key_bf = join_halves(key_bf, other_key, odd_flag)
        value_bf = join_halves(value_bf, other_value, odd_flag)
    pieces = (
        lax.all_gather(query_bf, "dp", axis=0, tiled=True),
        lax.all_gather(key_bf, "dp", axis=0, tiled=True),
        lax.all_gather(value_bf, "dp", axis=0, tiled=True),
    )
    columns = normed
    raw_q, raw_k, raw_v = tuple(
        (jnp.dot(columns, piece, preferred_element_type=jnp.float32) for piece in pieces)
    )
    head_size = raw_k.shape[1]
    local_heads = raw_q.shape[1] // head_size
    positions = jnp.arange(group_tokens, dtype=jnp.int32) % slot
    row_len = jnp.repeat(lengths, slot, total_repeat_length=group_tokens)
    live = positions < row_len
    queries = rotate_pairs(raw_q.reshape(group_tokens, local_heads, head_size), positions).astype(
        jnp.bfloat16
    )
    keys_rot = rotate_pairs(raw_k.reshape(group_tokens, 1, head_size), positions).reshape(
        group_tokens, head_size
    )
    keys_rot = jnp.where(live[:, None], keys_rot, jnp.float32(0.0)).astype(jnp.bfloat16)
    values_all = jnp.where(live[:, None], raw_v, jnp.float32(0.0)).astype(jnp.bfloat16)
    key_rows = keys_rot[0:slot]
    value_rows = values_all[0:slot]
    length = lengths[0]
    mixed = head_block(queries, key_rows, value_rows, slot, length)
    slot_pos = jnp.arange(slot, dtype=jnp.int32)
    mixed = jnp.where((slot_pos < length)[:, None, None], mixed, jnp.float32(0.0))
    attended_list = mixed.astype(jnp.bfloat16).reshape(slot, local_heads * head_size)
    attn_rows = lax.psum_scatter(
        jnp.dot(attended_list, output_weight, preferred_element_type=jnp.float32).astype(
            jnp.bfloat16
        ),
        "mp",
        scatter_dimension=0,
        tiled=True,
    ).astype(jnp.float32)
    residual = (inputs.astype(jnp.float32) + rms_norm(attn_rows, gain_post)).astype(jnp.bfloat16)
    pre_local = rms_norm(residual.astype(jnp.float32), gain_pre).astype(jnp.bfloat16)
    pre_ffn = lax.all_gather(pre_local, "mp", axis=0, tiled=True)
    pieces = (
        lax.all_gather(gate_bf, "dp", axis=0, tiled=True),
        lax.all_gather(up_bf, "dp", axis=0, tiled=True),
    )
    columns = pre_ffn
    gate = jnp.dot(columns, pieces[0], preferred_element_type=jnp.float32)
    up_part = jnp.dot(columns, pieces[1], preferred_element_type=jnp.float32)
    hidden = (jax.nn.gelu(gate, approximate=True) * up_part).astype(jnp.bfloat16)
    if paired:
        offset = mp_index % 2 * own_width
        keys_out = lax.dynamic_slice_in_dim(keys_rot, offset, own_width, 1)
        values_out = lax.dynamic_slice_in_dim(values_all, offset, own_width, 1)
    else:
        keys_out = keys_rot
        values_out = values_all
    return (residual, hidden, keys_out, values_out)


def swap_dp(value):
    return lax.ppermute(value, "dp", [(0, 1), (1, 0)])


def place_of():
    me = lax.axis_index("mp")
    return me, me // 4, (me // 2) % 2, me % 2


def index_of(z, y, core):
    return z * 4 + y * 2 + core


def greet(peers):
    barrier = pltpu.get_barrier_semaphore()
    for peer in peers:
        pl.semaphore_signal(barrier, inc=1, device_id=peer, device_id_type=pl.DeviceIdType.MESH)
    pl.semaphore_wait(barrier, len(peers))


def mp_peers():
    me, z, y, core = place_of()
    along_z = [{"mp": index_of(lax.rem(z + step, 4), y, core)} for step in (1, 2, 3)]
    return along_z, {"mp": index_of(z, 1 - y, core)}, {"mp": index_of(z, y, 1 - core)}


def gather_kernel(from_partner, block_ref, out_ref, send_sem, recv_sem):
    me, z, y, core = place_of()
    along_z, across_y, sibling = mp_peers()
    partner = {"dp": 1 - lax.axis_index("dp")}
    greet(along_z + [across_y, sibling] + ([partner] if from_partner else []))
    started = []

    def copy(source, slot, peer):
        return pltpu.make_async_remote_copy(
            src_ref=source,
            dst_ref=out_ref.at[slot],
            send_sem=send_sem.at[len(started)],
            recv_sem=recv_sem.at[slot],
            device_id=peer,
            device_id_type=pl.DeviceIdType.MESH,
        )

    def send(source, slot, peer):
        one = copy(source, slot, peer)
        one.start()
        started.append(one)

    def arrive(slot, peer):
        pltpu.make_async_remote_copy(
            src_ref=out_ref.at[slot],
            dst_ref=out_ref.at[slot],
            send_sem=send_sem.at[0],
            recv_sem=recv_sem.at[slot],
            device_id=peer,
            device_id_type=pl.DeviceIdType.MESH,
        ).wait_recv()

    if from_partner:
        send(block_ref, me, partner)
        arrive(me, partner)
    else:
        out_ref[me] = block_ref[...]
    mine = out_ref.at[me]
    for peer in along_z:
        send(mine, me, peer)
    send(mine, me, across_y)
    send(mine, me, sibling)
    for step in (1, 2, 3):
        slot = index_of(lax.rem(z + step, 4), y, core)
        arrive(slot, along_z[step - 1])
        send(out_ref.at[slot], slot, across_y)
        send(out_ref.at[slot], slot, sibling)
    for step in range(4):
        slot = index_of(lax.rem(z + step, 4), 1 - y, core)
        arrive(slot, across_y)
        send(out_ref.at[slot], slot, sibling)
    for step in range(4):
        for row in (y, 1 - y):
            arrive(index_of(lax.rem(z + step, 4), row, 1 - core), sibling)
    for one in started:
        one.wait_send()


def gather_mp(block, from_partner, collective_id):
    count = lax.axis_size("mp")
    rows, columns = block.shape
    out = pl.pallas_call(
        functools.partial(gather_kernel, from_partner),
        out_shape=jax.ShapeDtypeStruct((count, rows, columns), block.dtype),
        in_specs=[pl.BlockSpec(memory_space=pltpu.VMEM)],
        out_specs=pl.BlockSpec(memory_space=pltpu.VMEM),
        scratch_shapes=[
            pltpu.SemaphoreType.DMA((count,)),
            pltpu.SemaphoreType.DMA((count,)),
        ],
        compiler_params=pltpu.CompilerParams(
            collective_id=collective_id, has_side_effects=True, vmem_limit_bytes=32 * 2**20
        ),
        cost_estimate=pl.CostEstimate(flops=15 * 10**9, bytes_accessed=10**7, transcendentals=0),
    )(block)
    return out.reshape(count * rows, columns)


def scatter_kernel(
    part_ref, out_ref, core_buf, y_buf, z_buf, core_send, core_recv, y_send, y_recv, z_send, z_recv
):
    me, z, y, core = place_of()
    along_z, across_y, sibling = mp_peers()
    greet(along_z + [across_y, sibling])
    rows, columns = out_ref.shape
    width = columns // 9
    started = []

    def copy(source, target, send_sem, recv_sem, peer):
        return pltpu.make_async_remote_copy(
            src_ref=source,
            dst_ref=target,
            send_sem=send_sem,
            recv_sem=recv_sem,
            device_id=peer,
            device_id_type=pl.DeviceIdType.MESH,
        )

    def core_copy(zz, yy, target_core):
        place = zz * 2 + yy
        return copy(
            part_ref.at[index_of(zz, yy, target_core)],
            core_buf.at[place],
            core_send.at[place],
            core_recv.at[place],
            sibling,
        )

    order = [lax.rem(z + step, 4) for step in (2, 1, 3, 0)]
    for yy in (1 - y, y):
        for zz in order:
            one = core_copy(zz, yy, 1 - core)
            one.start()
            started.append(one)

    def add_core(zz, yy):
        core_copy(zz, yy, core).wait_recv()
        place, slot = zz * 2 + yy, index_of(zz, yy, core)
        for start in range(0, columns, width):
            cut = pl.ds(start, width)
            total = core_buf[place, :, cut].astype(jnp.float32) + part_ref[slot, :, cut].astype(
                jnp.float32
            )
            core_buf[place, :, cut] = total.astype(core_buf.dtype)

    def y_copy(zz, yy):
        return copy(
            core_buf.at[zz * 2 + yy], y_buf.at[zz], y_send.at[zz], y_recv.at[zz], across_y
        )

    for zz in order:
        add_core(zz, 1 - y)
        one = y_copy(zz, 1 - y)
        one.start()
        started.append(one)

    def z_copy(zz, source_z, peer):
        return copy(
            core_buf.at[zz * 2 + y],
            z_buf.at[source_z],
            z_send.at[zz],
            z_recv.at[source_z],
            peer,
        )

    for step in (2, 1, 3, 0):
        zz = lax.rem(z + step, 4)
        add_core(zz, y)
        y_copy(zz, y).wait_recv()
        if step == 0:
            continue
        place = zz * 2 + y
        for start in range(0, columns, width):
            cut = pl.ds(start, width)
            total = core_buf[place, :, cut].astype(jnp.float32) + y_buf[zz, :, cut].astype(
                jnp.float32
            )
            core_buf[place, :, cut] = total.astype(core_buf.dtype)
        one = z_copy(zz, z, along_z[step - 1])
        one.start()
        started.append(one)
    for step in (1, 3, 2):
        zz = lax.rem(z + step, 4)
        z_copy(zz, zz, along_z[step - 1]).wait_recv()
    for start in range(0, columns, width):
        cut = pl.ds(start, width)
        total = core_buf[z * 2 + y, :, cut].astype(jnp.float32) + y_buf[z, :, cut].astype(
            jnp.float32
        )
        for step in (1, 2, 3):
            total = total + z_buf[lax.rem(z + step, 4), :, cut].astype(jnp.float32)
        out_ref[:, cut] = total
    for one in started:
        one.wait_send()


def scatter_mp(partial, collective_id):
    count = lax.axis_size("mp")
    tokens, columns = partial.shape
    rows = tokens // count
    dma = pltpu.SemaphoreType.DMA
    return pl.pallas_call(
        scatter_kernel,
        out_shape=jax.ShapeDtypeStruct((rows, columns), jnp.float32),
        in_specs=[pl.BlockSpec(memory_space=pltpu.VMEM)],
        out_specs=pl.BlockSpec(memory_space=pltpu.VMEM),
        scratch_shapes=[
            pltpu.VMEM((8, rows, columns), partial.dtype),
            pltpu.VMEM((4, rows, columns), partial.dtype),
            pltpu.VMEM((4, rows, columns), partial.dtype),
            dma((8,)),
            dma((8,)),
            dma((4,)),
            dma((4,)),
            dma((4,)),
            dma((4,)),
        ],
        compiler_params=pltpu.CompilerParams(
            collective_id=collective_id, has_side_effects=True, vmem_limit_bytes=40 * 2**20
        ),
        cost_estimate=pl.CostEstimate(flops=30 * 10**9, bytes_accessed=10**7, transcendentals=0),
    )(partial.reshape(count, rows, columns))


def split_rows(block):
    half = block.shape[1] // 2
    index = lax.axis_index("dp")
    own = lax.dynamic_slice_in_dim(block, index * half, half, 1)
    other = lax.dynamic_slice_in_dim(block, (1 - index) * half, half, 1)
    return own, other


def on_device_pair(
    inputs,
    lengths,
    gain_in,
    query_weight,
    key_weight,
    value_weight,
    output_weight,
    gain_post,
    gain_pre,
    gate_weight,
    up_weight,
):
    bf16 = jnp.bfloat16
    slot = inputs.shape[0] * lax.axis_size("mp")
    length = lengths[0]
    normed_local = rms_norm(inputs.astype(jnp.float32), gain_in).astype(bf16)
    own_rows, other_rows = split_rows(normed_local)
    partner_tokens = gather_mp(other_rows, True, 0)
    qkv_weight = jnp.concatenate([query_weight, key_weight, value_weight], axis=1).astype(bf16)
    head_size = key_weight.shape[1]
    local_heads = query_weight.shape[1] // head_size
    partner_part = jnp.dot(partner_tokens, qkv_weight, preferred_element_type=jnp.float32)
    partner_part = partner_part.astype(bf16)
    own_rows = lax.optimization_barrier((partner_part, own_rows))[1]
    arrived = swap_dp(partner_part)
    own_tokens = gather_mp(own_rows, False, 1)
    raw = jnp.dot(own_tokens, qkv_weight, preferred_element_type=jnp.float32)
    raw = raw + arrived.astype(jnp.float32)
    q_cols = local_heads * head_size
    raw_q, raw_k, raw_v = (
        raw[:, :q_cols],
        raw[:, q_cols : q_cols + head_size],
        raw[:, q_cols + head_size :],
    )
    positions = jnp.arange(slot, dtype=jnp.int32)
    live = positions < length
    queries = rotate_pairs(raw_q.reshape(slot, local_heads, head_size), positions).astype(bf16)
    keys_rot = rotate_pairs(raw_k.reshape(slot, 1, head_size), positions).reshape(slot, head_size)
    keys_rot = jnp.where(live[:, None], keys_rot, jnp.float32(0.0)).astype(bf16)
    values_all = jnp.where(live[:, None], raw_v, jnp.float32(0.0)).astype(bf16)
    mixed = head_block(queries, keys_rot, values_all, slot, length)
    mixed = jnp.where(live[:, None, None], mixed, jnp.float32(0.0))
    attended = mixed.astype(bf16).reshape(slot, local_heads * head_size)
    attn_rows = scatter_mp(
        jnp.dot(attended, output_weight, preferred_element_type=jnp.float32).astype(bf16), 2
    )
    residual = (inputs.astype(jnp.float32) + rms_norm(attn_rows, gain_post)).astype(bf16)
    pre_local = rms_norm(residual.astype(jnp.float32), gain_pre).astype(bf16)
    own_rows, other_rows = split_rows(pre_local)
    partner_tokens = gather_mp(other_rows, True, 3)
    columns = gate_weight.shape[1]
    width = 256
    weights = []
    parts = []
    for start in range(0, columns, width):
        pair = tuple(
            weight[:, start : start + width].astype(bf16) for weight in (gate_weight, up_weight)
        )
        weights.append(pair)
        parts.append(
            tuple(
                jnp.dot(partner_tokens, piece, preferred_element_type=jnp.float32).astype(bf16)
                for piece in pair
            )
        )
    own_rows = lax.optimization_barrier((parts, own_rows))[1]
    sent = [tuple(swap_dp(part) for part in pair) for pair in parts]
    own_tokens = gather_mp(own_rows, False, 4)
    hidden = []
    for pair, arrived in zip(weights, sent):
        gate, up_part = tuple(
            jnp.dot(own_tokens, piece, preferred_element_type=jnp.float32)
            + other.astype(jnp.float32)
            for piece, other in zip(pair, arrived)
        )
        hidden.append((jax.nn.gelu(gate, approximate=True) * up_part).astype(bf16))
    return (residual, jnp.concatenate(hidden, axis=1), keys_rot, values_all)


def solution(mesh):
    pair_form = mesh.shape["dp"] == 2 and mesh.shape["mp"] == KVH
    in_specs = (
        P(("dp", "mp"), None),
        P("dp"),
        P(),
        P("dp", "mp"),
        P("dp", "mp"),
        P("dp", "mp"),
        P("mp", None),
        P(),
        P(),
        P("dp", "mp"),
        P("dp", "mp"),
    )
    out_specs = (P(("dp", "mp"), None), P("dp", "mp"), P("dp", "mp"), P("dp", "mp"))
    return jax.shard_map(
        on_device_pair if pair_form else on_device, mesh=mesh, in_specs=in_specs, out_specs=out_specs, check_vma=False
    )
```

```python
import functools
import math

import jax
import jax.numpy as jnp
from jax import lax
from jax.experimental import pallas as pl
from jax.experimental.pallas import tpu as pltpu
from jax.sharding import PartitionSpec as P

KVH = 16


query_scale = 1.0 / 12.0
soft_cap = 50.0


def swapped(value, axis, stride):
    mask = 2**stride
    pairs = [(source, source ^ mask) for source in range(lax.axis_size(axis))]
    return lax.ppermute(value, axis, pairs)


def rms_norm(values, gain):
    mean_sq = jnp.mean(values * values, axis=-1, keepdims=True)
    return values * lax.rsqrt(mean_sq + 1e-06) * gain


def rotate_pairs(values, positions):
    half_size = values.shape[-1] // 2
    freqs = jnp.exp(
        jnp.arange(half_size, dtype=jnp.float32) * (-2.0 * math.log(10000.0) / values.shape[-1])
    )
    angles = positions.astype(jnp.float32)[:, None] * freqs[None, :]
    cosine = jnp.cos(angles)[:, None, :]
    sine = jnp.sin(angles)[:, None, :]
    first = values[..., :half_size]
    second = values[..., half_size:]
    return jnp.concatenate(
        [first * cosine - second * sine, second * cosine + first * sine], axis=-1
    )


def join_halves(own_half, other_half, odd_flag):
    lower_first = jnp.concatenate([own_half, other_half], axis=1)
    upper_first = jnp.concatenate([other_half, own_half], axis=1)
    return jnp.where(odd_flag, upper_first, lower_first)


def head_block(query_rows, key_rows, value_rows, key_count, length):
    scores = (
        jnp.einsum("qhd,kd->hqk", query_rows, key_rows, preferred_element_type=jnp.float32)
        * query_scale
    )
    capped = soft_cap * jnp.tanh(scores / soft_cap)
    query_pos = jnp.arange(query_rows.shape[0], dtype=jnp.int32)
    key_pos = jnp.arange(key_count, dtype=jnp.int32)
    allowed = (key_pos[None, :] <= query_pos[:, None]) & (key_pos[None, :] < length)
    weights_exp = jnp.where(allowed[None], jnp.exp(capped), jnp.float32(0.0))
    probs = (weights_exp / jnp.sum(weights_exp, axis=-1, keepdims=True)).astype(jnp.bfloat16)
    return jnp.einsum("hqk,kd->qhd", probs, value_rows, preferred_element_type=jnp.float32)


def on_device(
    inputs,
    lengths,
    gain_in,
    query_weight,
    key_weight,
    value_weight,
    output_weight,
    gain_post,
    gain_pre,
    gate_weight,
    up_weight,
):
    mp_count = lax.axis_size("mp")
    mp_index = lax.axis_index("mp")
    odd_flag = mp_index % 2 == 1
    paired = mp_count > KVH
    gate_bf = gate_weight.astype(jnp.bfloat16)
    up_bf = up_weight.astype(jnp.bfloat16)
    normed_local = rms_norm(inputs.astype(jnp.float32), gain_in).astype(jnp.bfloat16)
    normed = lax.all_gather(normed_local, "mp", axis=0, tiled=True)
    group_tokens = normed.shape[0]
    prompts = lengths.shape[0]
    slot = group_tokens // prompts
    query_bf = query_weight.astype(jnp.bfloat16)
    key_bf = key_weight.astype(jnp.bfloat16)
    value_bf = value_weight.astype(jnp.bfloat16)
    own_width = key_weight.shape[1]
    if paired:
        other_key, other_value = swapped((key_bf, value_bf), "mp", 0)
        key_bf = join_halves(key_bf, other_key, odd_flag)
        value_bf = join_halves(value_bf, other_value, odd_flag)
    pieces = (
        lax.all_gather(query_bf, "dp", axis=0, tiled=True),
        lax.all_gather(key_bf, "dp", axis=0, tiled=True),
        lax.all_gather(value_bf, "dp", axis=0, tiled=True),
    )
    columns = normed
    raw_q, raw_k, raw_v = tuple(
        (jnp.dot(columns, piece, preferred_element_type=jnp.float32) for piece in pieces)
    )
    head_size = raw_k.shape[1]
    local_heads = raw_q.shape[1] // head_size
    positions = jnp.arange(group_tokens, dtype=jnp.int32) % slot
    row_len = jnp.repeat(lengths, slot, total_repeat_length=group_tokens)
    live = positions < row_len
    queries = rotate_pairs(raw_q.reshape(group_tokens, local_heads, head_size), positions).astype(
        jnp.bfloat16
    )
    keys_rot = rotate_pairs(raw_k.reshape(group_tokens, 1, head_size), positions).reshape(
        group_tokens, head_size
    )
    keys_rot = jnp.where(live[:, None], keys_rot, jnp.float32(0.0)).astype(jnp.bfloat16)
    values_all = jnp.where(live[:, None], raw_v, jnp.float32(0.0)).astype(jnp.bfloat16)
    key_rows = keys_rot[0:slot]
    value_rows = values_all[0:slot]
    length = lengths[0]
    mixed = head_block(queries, key_rows, value_rows, slot, length)
    slot_pos = jnp.arange(slot, dtype=jnp.int32)
    mixed = jnp.where((slot_pos < length)[:, None, None], mixed, jnp.float32(0.0))
    attended_list = mixed.astype(jnp.bfloat16).reshape(slot, local_heads * head_size)
    attn_rows = lax.psum_scatter(
        jnp.dot(attended_list, output_weight, preferred_element_type=jnp.float32).astype(
            jnp.bfloat16
        ),
        "mp",
        scatter_dimension=0,
        tiled=True,
    ).astype(jnp.float32)
    residual = (inputs.astype(jnp.float32) + rms_norm(attn_rows, gain_post)).astype(jnp.bfloat16)
    pre_local = rms_norm(residual.astype(jnp.float32), gain_pre).astype(jnp.bfloat16)
    pre_ffn = lax.all_gather(pre_local, "mp", axis=0, tiled=True)
    pieces = (
        lax.all_gather(gate_bf, "dp", axis=0, tiled=True),
        lax.all_gather(up_bf, "dp", axis=0, tiled=True),
    )
    columns = pre_ffn
    gate = jnp.dot(columns, pieces[0], preferred_element_type=jnp.float32)
    up_part = jnp.dot(columns, pieces[1], preferred_element_type=jnp.float32)
    hidden = (jax.nn.gelu(gate, approximate=True) * up_part).astype(jnp.bfloat16)
    if paired:
        offset = mp_index % 2 * own_width
        keys_out = lax.dynamic_slice_in_dim(keys_rot, offset, own_width, 1)
        values_out = lax.dynamic_slice_in_dim(values_all, offset, own_width, 1)
    else:
        keys_out = keys_rot
        values_out = values_all
    return (residual, hidden, keys_out, values_out)


def swap_dp(value):
    return lax.ppermute(value, "dp", [(0, 1), (1, 0)])


def place_of():
    me = lax.axis_index("mp")
    return me, me // 4, (me // 2) % 2, me % 2


def index_of(z, y, core):
    return z * 4 + y * 2 + core


def greet(peers):
    barrier = pltpu.get_barrier_semaphore()
    for peer in peers:
        pl.semaphore_signal(barrier, inc=1, device_id=peer, device_id_type=pl.DeviceIdType.MESH)
    pl.semaphore_wait(barrier, len(peers))


def mp_peers():
    me, z, y, core = place_of()
    along_z = [{"mp": index_of(lax.rem(z + step, 4), y, core)} for step in (1, 2, 3)]
    return along_z, {"mp": index_of(z, 1 - y, core)}, {"mp": index_of(z, y, 1 - core)}


def gather_kernel(
    from_partner, block_ref, out_ref, x_send, up_send, down_send, y_send, core_send, recv_sem
):
    me, z, y, core = place_of()
    _, across_y, sibling = mp_peers()
    partner = {"dp": 1 - lax.axis_index("dp")}
    above = {"mp": index_of(lax.rem(z + 1, 4), y, core)}
    below = {"mp": index_of(lax.rem(z + 3, 4), y, core)}
    has_above, has_below = z < 3, z > 0
    barrier = pltpu.get_barrier_semaphore()

    def greet_one(peer):
        pl.semaphore_signal(barrier, inc=1, device_id=peer, device_id_type=pl.DeviceIdType.MESH)

    greet_one(across_y)
    greet_one(sibling)
    if from_partner:
        greet_one(partner)
    pl.when(has_above)(lambda: greet_one(above))
    pl.when(has_below)(lambda: greet_one(below))
    inner = has_above.astype(jnp.int32) + has_below.astype(jnp.int32)
    pl.semaphore_wait(barrier, (3 if from_partner else 2) + inner)

    def copy(slot, send_sem, peer, source=None):
        return pltpu.make_async_remote_copy(
            src_ref=out_ref.at[slot] if source is None else source,
            dst_ref=out_ref.at[slot],
            send_sem=send_sem,
            recv_sem=recv_sem.at[slot],
            device_id=peer,
            device_id_type=pl.DeviceIdType.MESH,
        )

    def column_slot(zz):
        return index_of(zz, y, core)

    def y_copy(zz):
        return copy(column_slot(zz), y_send.at[zz], across_y)

    def core_copy(zz, yy):
        return copy(index_of(zz, yy, core), core_send.at[zz * 2 + yy], sibling)

    def up_copy(step):
        return copy(column_slot(z - step), up_send.at[step], above)

    def down_copy(step):
        return copy(column_slot(z + step), down_send.at[step], below)

    if from_partner:
        exchange = copy(me, x_send, partner, block_ref)
        exchange.start()
        exchange.wait()
    else:
        out_ref[me] = block_ref[...]
    pl.when(has_above)(lambda: up_copy(0).start())
    pl.when(has_below)(lambda: down_copy(0).start())
    y_copy(z).start()
    core_copy(z, y).start()
    for step in (1, 2, 3):

        @pl.when(z >= step)
        def _():
            copy(column_slot(z - step), y_send.at[0], below).wait_recv()
            if step < 3:
                pl.when(has_above)(lambda: up_copy(step).start())
            y_copy(z - step).start()
            core_copy(z - step, y).start()

        @pl.when(z + step <= 3)
        def _():
            copy(column_slot(z + step), y_send.at[0], above).wait_recv()
            if step < 3:
                pl.when(has_below)(lambda: down_copy(step).start())
            y_copy(z + step).start()
            core_copy(z + step, y).start()

    for step in range(4):
        zz = lax.rem(z + step, 4)
        copy(index_of(zz, 1 - y, core), y_send.at[0], across_y).wait_recv()
        core_copy(zz, 1 - y).start()
    for zz in range(4):
        for yy in range(2):
            copy(index_of(zz, yy, 1 - core), y_send.at[0], sibling).wait_recv()
    for step in (0, 1, 2):
        pl.when(jnp.logical_and(has_above, z >= step))(lambda: up_copy(step).wait_send())
        pl.when(jnp.logical_and(has_below, z + step <= 3))(lambda: down_copy(step).wait_send())
    for zz in range(4):
        y_copy(zz).wait_send()
        for yy in range(2):
            core_copy(zz, yy).wait_send()


def gather_mp(block, from_partner, collective_id):
    count = lax.axis_size("mp")
    rows, columns = block.shape
    out = pl.pallas_call(
        functools.partial(gather_kernel, from_partner),
        out_shape=jax.ShapeDtypeStruct((count, rows, columns), block.dtype),
        in_specs=[pl.BlockSpec(memory_space=pltpu.VMEM)],
        out_specs=pl.BlockSpec(memory_space=pltpu.VMEM),
        scratch_shapes=[
            pltpu.SemaphoreType.DMA(()),
            pltpu.SemaphoreType.DMA((3,)),
            pltpu.SemaphoreType.DMA((3,)),
            pltpu.SemaphoreType.DMA((4,)),
            pltpu.SemaphoreType.DMA((8,)),
            pltpu.SemaphoreType.DMA((count,)),
        ],
        compiler_params=pltpu.CompilerParams(
            collective_id=collective_id, has_side_effects=True, vmem_limit_bytes=32 * 2**20
        ),
        cost_estimate=pl.CostEstimate(flops=15 * 10**9, bytes_accessed=10**7, transcendentals=0),
    )(block)
    return out.reshape(count * rows, columns)


def scatter_kernel(
    part_ref, out_ref, core_buf, y_buf, z_buf, core_send, core_recv, y_send, y_recv, z_send, z_recv
):
    me, z, y, core = place_of()
    along_z, across_y, sibling = mp_peers()
    greet(along_z + [across_y, sibling])
    rows, columns = out_ref.shape
    width = columns // 9
    started = []

    def copy(source, target, send_sem, recv_sem, peer):
        return pltpu.make_async_remote_copy(
            src_ref=source,
            dst_ref=target,
            send_sem=send_sem,
            recv_sem=recv_sem,
            device_id=peer,
            device_id_type=pl.DeviceIdType.MESH,
        )

    def core_copy(zz, yy, target_core):
        place = zz * 2 + yy
        return copy(
            part_ref.at[index_of(zz, yy, target_core)],
            core_buf.at[place],
            core_send.at[place],
            core_recv.at[place],
            sibling,
        )

    order = [lax.rem(z + step, 4) for step in (2, 1, 3, 0)]
    for yy in (1 - y, y):
        for zz in order:
            one = core_copy(zz, yy, 1 - core)
            one.start()
            started.append(one)

    def add_core(zz, yy):
        core_copy(zz, yy, core).wait_recv()
        place, slot = zz * 2 + yy, index_of(zz, yy, core)
        for start in range(0, columns, width):
            cut = pl.ds(start, width)
            total = core_buf[place, :, cut].astype(jnp.float32) + part_ref[slot, :, cut].astype(
                jnp.float32
            )
            core_buf[place, :, cut] = total.astype(core_buf.dtype)

    def y_copy(zz, yy):
        return copy(
            core_buf.at[zz * 2 + yy], y_buf.at[zz], y_send.at[zz], y_recv.at[zz], across_y
        )

    for zz in order:
        add_core(zz, 1 - y)
        one = y_copy(zz, 1 - y)
        one.start()
        started.append(one)

    def z_copy(zz, source_z, peer):
        return copy(
            core_buf.at[zz * 2 + y],
            z_buf.at[source_z],
            z_send.at[zz],
            z_recv.at[source_z],
            peer,
        )

    for step in (2, 1, 3, 0):
        zz = lax.rem(z + step, 4)
        add_core(zz, y)
        y_copy(zz, y).wait_recv()
        if step == 0:
            continue
        place = zz * 2 + y
        for start in range(0, columns, width):
            cut = pl.ds(start, width)
            total = core_buf[place, :, cut].astype(jnp.float32) + y_buf[zz, :, cut].astype(
                jnp.float32
            )
            core_buf[place, :, cut] = total.astype(core_buf.dtype)
        one = z_copy(zz, z, along_z[step - 1])
        one.start()
        started.append(one)
    for step in (1, 3, 2):
        zz = lax.rem(z + step, 4)
        z_copy(zz, zz, along_z[step - 1]).wait_recv()
    for start in range(0, columns, width):
        cut = pl.ds(start, width)
        total = core_buf[z * 2 + y, :, cut].astype(jnp.float32) + y_buf[z, :, cut].astype(
            jnp.float32
        )
        for step in (1, 2, 3):
            total = total + z_buf[lax.rem(z + step, 4), :, cut].astype(jnp.float32)
        out_ref[:, cut] = total
    for one in started:
        one.wait_send()


def scatter_mp(partial, collective_id):
    count = lax.axis_size("mp")
    tokens, columns = partial.shape
    rows = tokens // count
    dma = pltpu.SemaphoreType.DMA
    return pl.pallas_call(
        scatter_kernel,
        out_shape=jax.ShapeDtypeStruct((rows, columns), jnp.float32),
        in_specs=[pl.BlockSpec(memory_space=pltpu.VMEM)],
        out_specs=pl.BlockSpec(memory_space=pltpu.VMEM),
        scratch_shapes=[
            pltpu.VMEM((8, rows, columns), partial.dtype),
            pltpu.VMEM((4, rows, columns), partial.dtype),
            pltpu.VMEM((4, rows, columns), partial.dtype),
            dma((8,)),
            dma((8,)),
            dma((4,)),
            dma((4,)),
            dma((4,)),
            dma((4,)),
        ],
        compiler_params=pltpu.CompilerParams(
            collective_id=collective_id, has_side_effects=True, vmem_limit_bytes=40 * 2**20
        ),
        cost_estimate=pl.CostEstimate(flops=30 * 10**9, bytes_accessed=10**7, transcendentals=0),
    )(partial.reshape(count, rows, columns))


def split_rows(block):
    half = block.shape[1] // 2
    index = lax.axis_index("dp")
    own = lax.dynamic_slice_in_dim(block, index * half, half, 1)
    other = lax.dynamic_slice_in_dim(block, (1 - index) * half, half, 1)
    return own, other


def on_device_pair(
    inputs,
    lengths,
    gain_in,
    query_weight,
    key_weight,
    value_weight,
    output_weight,
    gain_post,
    gain_pre,
    gate_weight,
    up_weight,
):
    bf16 = jnp.bfloat16
    slot = inputs.shape[0] * lax.axis_size("mp")
    length = lengths[0]
    normed_local = rms_norm(inputs.astype(jnp.float32), gain_in).astype(bf16)
    own_rows, other_rows = split_rows(normed_local)
    partner_tokens = gather_mp(other_rows, True, 0)
    qkv_weight = jnp.concatenate([query_weight, key_weight, value_weight], axis=1).astype(bf16)
    head_size = key_weight.shape[1]
    local_heads = query_weight.shape[1] // head_size
    partner_part = jnp.dot(partner_tokens, qkv_weight, preferred_element_type=jnp.float32)
    partner_part = partner_part.astype(bf16)
    own_rows = lax.optimization_barrier((partner_part, own_rows))[1]
    arrived = swap_dp(partner_part)
    own_tokens = gather_mp(own_rows, False, 1)
    raw = jnp.dot(own_tokens, qkv_weight, preferred_element_type=jnp.float32)
    raw = raw + arrived.astype(jnp.float32)
    q_cols = local_heads * head_size
    raw_q, raw_k, raw_v = (
        raw[:, :q_cols],
        raw[:, q_cols : q_cols + head_size],
        raw[:, q_cols + head_size :],
    )
    positions = jnp.arange(slot, dtype=jnp.int32)
    live = positions < length
    queries = rotate_pairs(raw_q.reshape(slot, local_heads, head_size), positions).astype(bf16)
    keys_rot = rotate_pairs(raw_k.reshape(slot, 1, head_size), positions).reshape(slot, head_size)
    keys_rot = jnp.where(live[:, None], keys_rot, jnp.float32(0.0)).astype(bf16)
    values_all = jnp.where(live[:, None], raw_v, jnp.float32(0.0)).astype(bf16)
    mixed = head_block(queries, keys_rot, values_all, slot, length)
    mixed = jnp.where(live[:, None, None], mixed, jnp.float32(0.0))
    attended = mixed.astype(bf16).reshape(slot, local_heads * head_size)
    attn_rows = scatter_mp(
        jnp.dot(attended, output_weight, preferred_element_type=jnp.float32).astype(bf16), 2
    )
    residual = (inputs.astype(jnp.float32) + rms_norm(attn_rows, gain_post)).astype(bf16)
    pre_local = rms_norm(residual.astype(jnp.float32), gain_pre).astype(bf16)
    own_rows, other_rows = split_rows(pre_local)
    partner_tokens = gather_mp(other_rows, True, 3)
    columns = gate_weight.shape[1]
    width = columns // 2
    early_weights = lax.optimization_barrier((gate_weight, up_weight, partner_tokens))[:2]
    cuts = range(0, columns, width)
    parts = [
        tuple(
            jnp.dot(
                partner_tokens,
                weight[:, start : start + width].astype(bf16),
                preferred_element_type=jnp.float32,
            ).astype(bf16)
            for weight in early_weights
        )
        for start in cuts
    ]
    own_rows = lax.optimization_barrier((parts, own_rows))[1]
    sent = [tuple(swap_dp(part) for part in pair) for pair in parts]
    own_tokens = gather_mp(own_rows, False, 4)
    late_weights = lax.optimization_barrier((gate_weight, up_weight, own_tokens))[:2]
    products = [
        tuple(
            jnp.dot(
                own_tokens,
                weight[:, start : start + width].astype(bf16),
                preferred_element_type=jnp.float32,
            )
            for weight in late_weights
        )
        for start in cuts
    ]
    hidden = []
    for pair, arrived in zip(products, sent):
        gate, up_part = tuple(
            piece + other.astype(jnp.float32) for piece, other in zip(pair, arrived)
        )
        hidden.append((jax.nn.gelu(gate, approximate=True) * up_part).astype(bf16))
    return (residual, jnp.concatenate(hidden, axis=1), keys_rot, values_all)


def solution(mesh):
    pair_form = mesh.shape["dp"] == 2 and mesh.shape["mp"] == KVH
    in_specs = (
        P(("dp", "mp"), None),
        P("dp"),
        P(),
        P("dp", "mp"),
        P("dp", "mp"),
        P("dp", "mp"),
        P("mp", None),
        P(),
        P(),
        P("dp", "mp"),
        P("dp", "mp"),
    )
    out_specs = (P(("dp", "mp"), None), P("dp", "mp"), P("dp", "mp"), P("dp", "mp"))
    return jax.shard_map(
        on_device_pair if pair_form else on_device, mesh=mesh, in_specs=in_specs, out_specs=out_specs, check_vma=False
    )
```

```python
import functools
import math

import jax
import jax.numpy as jnp
from jax import lax
from jax.experimental import pallas as pl
from jax.experimental.pallas import tpu as pltpu
from jax.sharding import PartitionSpec as P

KVH = 16


query_scale = 1.0 / 12.0
soft_cap = 50.0


def swapped(value, axis, stride):
    mask = 2**stride
    pairs = [(source, source ^ mask) for source in range(lax.axis_size(axis))]
    return lax.ppermute(value, axis, pairs)


def rms_norm(values, gain):
    mean_sq = jnp.mean(values * values, axis=-1, keepdims=True)
    return values * lax.rsqrt(mean_sq + 1e-06) * gain


def rotate_pairs(values, positions):
    half_size = values.shape[-1] // 2
    freqs = jnp.exp(
        jnp.arange(half_size, dtype=jnp.float32) * (-2.0 * math.log(10000.0) / values.shape[-1])
    )
    angles = positions.astype(jnp.float32)[:, None] * freqs[None, :]
    cosine = jnp.cos(angles)[:, None, :]
    sine = jnp.sin(angles)[:, None, :]
    first = values[..., :half_size]
    second = values[..., half_size:]
    return jnp.concatenate(
        [first * cosine - second * sine, second * cosine + first * sine], axis=-1
    )


def join_halves(own_half, other_half, odd_flag):
    lower_first = jnp.concatenate([own_half, other_half], axis=1)
    upper_first = jnp.concatenate([other_half, own_half], axis=1)
    return jnp.where(odd_flag, upper_first, lower_first)


def head_block(query_rows, key_rows, value_rows, key_count, length):
    scores = (
        jnp.einsum("qhd,kd->hqk", query_rows, key_rows, preferred_element_type=jnp.float32)
        * query_scale
    )
    capped = soft_cap * jnp.tanh(scores / soft_cap)
    query_pos = jnp.arange(query_rows.shape[0], dtype=jnp.int32)
    key_pos = jnp.arange(key_count, dtype=jnp.int32)
    allowed = (key_pos[None, :] <= query_pos[:, None]) & (key_pos[None, :] < length)
    weights_exp = jnp.where(allowed[None], jnp.exp(capped), jnp.float32(0.0))
    probs = (weights_exp / jnp.sum(weights_exp, axis=-1, keepdims=True)).astype(jnp.bfloat16)
    return jnp.einsum("hqk,kd->qhd", probs, value_rows, preferred_element_type=jnp.float32)


def on_device(
    inputs,
    lengths,
    gain_in,
    query_weight,
    key_weight,
    value_weight,
    output_weight,
    gain_post,
    gain_pre,
    gate_weight,
    up_weight,
):
    mp_count = lax.axis_size("mp")
    mp_index = lax.axis_index("mp")
    odd_flag = mp_index % 2 == 1
    paired = mp_count > KVH
    gate_bf = gate_weight.astype(jnp.bfloat16)
    up_bf = up_weight.astype(jnp.bfloat16)
    normed_local = rms_norm(inputs.astype(jnp.float32), gain_in).astype(jnp.bfloat16)
    normed = lax.all_gather(normed_local, "mp", axis=0, tiled=True)
    group_tokens = normed.shape[0]
    prompts = lengths.shape[0]
    slot = group_tokens // prompts
    query_bf = query_weight.astype(jnp.bfloat16)
    key_bf = key_weight.astype(jnp.bfloat16)
    value_bf = value_weight.astype(jnp.bfloat16)
    own_width = key_weight.shape[1]
    if paired:
        other_key, other_value = swapped((key_bf, value_bf), "mp", 0)
        key_bf = join_halves(key_bf, other_key, odd_flag)
        value_bf = join_halves(value_bf, other_value, odd_flag)
    pieces = (
        lax.all_gather(query_bf, "dp", axis=0, tiled=True),
        lax.all_gather(key_bf, "dp", axis=0, tiled=True),
        lax.all_gather(value_bf, "dp", axis=0, tiled=True),
    )
    columns = normed
    raw_q, raw_k, raw_v = tuple(
        (jnp.dot(columns, piece, preferred_element_type=jnp.float32) for piece in pieces)
    )
    head_size = raw_k.shape[1]
    local_heads = raw_q.shape[1] // head_size
    positions = jnp.arange(group_tokens, dtype=jnp.int32) % slot
    row_len = jnp.repeat(lengths, slot, total_repeat_length=group_tokens)
    live = positions < row_len
    queries = rotate_pairs(raw_q.reshape(group_tokens, local_heads, head_size), positions).astype(
        jnp.bfloat16
    )
    keys_rot = rotate_pairs(raw_k.reshape(group_tokens, 1, head_size), positions).reshape(
        group_tokens, head_size
    )
    keys_rot = jnp.where(live[:, None], keys_rot, jnp.float32(0.0)).astype(jnp.bfloat16)
    values_all = jnp.where(live[:, None], raw_v, jnp.float32(0.0)).astype(jnp.bfloat16)
    key_rows = keys_rot[0:slot]
    value_rows = values_all[0:slot]
    length = lengths[0]
    mixed = head_block(queries, key_rows, value_rows, slot, length)
    slot_pos = jnp.arange(slot, dtype=jnp.int32)
    mixed = jnp.where((slot_pos < length)[:, None, None], mixed, jnp.float32(0.0))
    attended_list = mixed.astype(jnp.bfloat16).reshape(slot, local_heads * head_size)
    attn_rows = lax.psum_scatter(
        jnp.dot(attended_list, output_weight, preferred_element_type=jnp.float32).astype(
            jnp.bfloat16
        ),
        "mp",
        scatter_dimension=0,
        tiled=True,
    ).astype(jnp.float32)
    residual = (inputs.astype(jnp.float32) + rms_norm(attn_rows, gain_post)).astype(jnp.bfloat16)
    pre_local = rms_norm(residual.astype(jnp.float32), gain_pre).astype(jnp.bfloat16)
    pre_ffn = lax.all_gather(pre_local, "mp", axis=0, tiled=True)
    pieces = (
        lax.all_gather(gate_bf, "dp", axis=0, tiled=True),
        lax.all_gather(up_bf, "dp", axis=0, tiled=True),
    )
    columns = pre_ffn
    gate = jnp.dot(columns, pieces[0], preferred_element_type=jnp.float32)
    up_part = jnp.dot(columns, pieces[1], preferred_element_type=jnp.float32)
    hidden = (jax.nn.gelu(gate, approximate=True) * up_part).astype(jnp.bfloat16)
    if paired:
        offset = mp_index % 2 * own_width
        keys_out = lax.dynamic_slice_in_dim(keys_rot, offset, own_width, 1)
        values_out = lax.dynamic_slice_in_dim(values_all, offset, own_width, 1)
    else:
        keys_out = keys_rot
        values_out = values_all
    return (residual, hidden, keys_out, values_out)


def swap_dp(value):
    return lax.ppermute(value, "dp", [(0, 1), (1, 0)])


def place_of():
    me = lax.axis_index("mp")
    return me, me // 4, (me // 2) % 2, me % 2


def index_of(z, y, core):
    return z * 4 + y * 2 + core


def greet(peers):
    barrier = pltpu.get_barrier_semaphore()
    for peer in peers:
        pl.semaphore_signal(barrier, inc=1, device_id=peer, device_id_type=pl.DeviceIdType.MESH)
    pl.semaphore_wait(barrier, len(peers))


def mp_peers():
    me, z, y, core = place_of()
    along_z = [{"mp": index_of(lax.rem(z + step, 4), y, core)} for step in (1, 2, 3)]
    return along_z, {"mp": index_of(z, 1 - y, core)}, {"mp": index_of(z, y, 1 - core)}


def gather_kernel(
    from_partner, block_ref, out_ref, x_send, up_send, down_send, y_send, core_send, recv_sem
):
    me, z, y, core = place_of()
    _, across_y, sibling = mp_peers()
    partner = {"dp": 1 - lax.axis_index("dp")}
    above = {"mp": index_of(lax.rem(z + 1, 4), y, core)}
    below = {"mp": index_of(lax.rem(z + 3, 4), y, core)}
    has_above, has_below = z < 3, z > 0
    barrier = pltpu.get_barrier_semaphore()

    def greet_one(peer):
        pl.semaphore_signal(barrier, inc=1, device_id=peer, device_id_type=pl.DeviceIdType.MESH)

    greet_one(across_y)
    greet_one(sibling)
    if from_partner:
        greet_one(partner)
    pl.when(has_above)(lambda: greet_one(above))
    pl.when(has_below)(lambda: greet_one(below))
    inner = has_above.astype(jnp.int32) + has_below.astype(jnp.int32)
    pl.semaphore_wait(barrier, (3 if from_partner else 2) + inner)

    def copy(slot, send_sem, peer, source=None):
        return pltpu.make_async_remote_copy(
            src_ref=out_ref.at[slot] if source is None else source,
            dst_ref=out_ref.at[slot],
            send_sem=send_sem,
            recv_sem=recv_sem.at[slot],
            device_id=peer,
            device_id_type=pl.DeviceIdType.MESH,
        )

    def column_slot(zz):
        return index_of(zz, y, core)

    def y_copy(zz):
        return copy(column_slot(zz), y_send.at[zz], across_y)

    def core_copy(zz, yy):
        return copy(index_of(zz, yy, core), core_send.at[zz * 2 + yy], sibling)

    def up_copy(step):
        return copy(column_slot(z - step), up_send.at[step], above)

    def down_copy(step):
        return copy(column_slot(z + step), down_send.at[step], below)

    if from_partner:
        exchange = copy(me, x_send, partner, block_ref)
        exchange.start()
        exchange.wait()
    else:
        out_ref[me] = block_ref[...]
    pl.when(has_above)(lambda: up_copy(0).start())
    pl.when(has_below)(lambda: down_copy(0).start())
    y_copy(z).start()
    core_copy(z, y).start()
    for step in (1, 2, 3):

        @pl.when(z >= step)
        def _():
            copy(column_slot(z - step), y_send.at[0], below).wait_recv()
            if step < 3:
                pl.when(has_above)(lambda: up_copy(step).start())
            y_copy(z - step).start()
            core_copy(z - step, y).start()

        @pl.when(z + step <= 3)
        def _():
            copy(column_slot(z + step), y_send.at[0], above).wait_recv()
            if step < 3:
                pl.when(has_below)(lambda: down_copy(step).start())
            y_copy(z + step).start()
            core_copy(z + step, y).start()

    for step in range(4):
        zz = lax.rem(z + step, 4)
        copy(index_of(zz, 1 - y, core), y_send.at[0], across_y).wait_recv()
        core_copy(zz, 1 - y).start()
    for zz in range(4):
        for yy in range(2):
            copy(index_of(zz, yy, 1 - core), y_send.at[0], sibling).wait_recv()
    for step in (0, 1, 2):
        pl.when(jnp.logical_and(has_above, z >= step))(lambda: up_copy(step).wait_send())
        pl.when(jnp.logical_and(has_below, z + step <= 3))(lambda: down_copy(step).wait_send())
    for zz in range(4):
        y_copy(zz).wait_send()
        for yy in range(2):
            core_copy(zz, yy).wait_send()


def gather_mp(block, from_partner, collective_id):
    count = lax.axis_size("mp")
    rows, columns = block.shape
    out = pl.pallas_call(
        functools.partial(gather_kernel, from_partner),
        out_shape=jax.ShapeDtypeStruct((count, rows, columns), block.dtype),
        in_specs=[pl.BlockSpec(memory_space=pltpu.VMEM)],
        out_specs=pl.BlockSpec(memory_space=pltpu.VMEM),
        scratch_shapes=[
            pltpu.SemaphoreType.DMA(()),
            pltpu.SemaphoreType.DMA((3,)),
            pltpu.SemaphoreType.DMA((3,)),
            pltpu.SemaphoreType.DMA((4,)),
            pltpu.SemaphoreType.DMA((8,)),
            pltpu.SemaphoreType.DMA((count,)),
        ],
        compiler_params=pltpu.CompilerParams(
            collective_id=collective_id, has_side_effects=True, vmem_limit_bytes=32 * 2**20
        ),
        cost_estimate=pl.CostEstimate(flops=10**9, bytes_accessed=10**6, transcendentals=0),
    )(block)
    return out.reshape(count * rows, columns)


def scatter_kernel(
    part_ref, out_ref, core_buf, y_buf, z_buf, core_send, core_recv, y_send, y_recv, z_send, z_recv
):
    me, z, y, core = place_of()
    along_z, across_y, sibling = mp_peers()
    greet(along_z + [across_y, sibling])
    rows, columns = out_ref.shape
    width = columns // 9
    started = []

    def copy(source, target, send_sem, recv_sem, peer):
        return pltpu.make_async_remote_copy(
            src_ref=source,
            dst_ref=target,
            send_sem=send_sem,
            recv_sem=recv_sem,
            device_id=peer,
            device_id_type=pl.DeviceIdType.MESH,
        )

    def core_copy(zz, yy, target_core):
        place = zz * 2 + yy
        return copy(
            part_ref.at[index_of(zz, yy, target_core)],
            core_buf.at[place],
            core_send.at[place],
            core_recv.at[place],
            sibling,
        )

    order = [lax.rem(z + step, 4) for step in (2, 1, 3, 0)]
    for yy in (1 - y, y):
        for zz in order:
            one = core_copy(zz, yy, 1 - core)
            one.start()
            started.append(one)

    def add_core(zz, yy):
        core_copy(zz, yy, core).wait_recv()
        place, slot = zz * 2 + yy, index_of(zz, yy, core)
        for start in range(0, columns, width):
            cut = pl.ds(start, width)
            total = core_buf[place, :, cut].astype(jnp.float32) + part_ref[slot, :, cut].astype(
                jnp.float32
            )
            core_buf[place, :, cut] = total.astype(core_buf.dtype)

    def y_copy(zz, yy):
        return copy(
            core_buf.at[zz * 2 + yy], y_buf.at[zz], y_send.at[zz], y_recv.at[zz], across_y
        )

    for zz in order:
        add_core(zz, 1 - y)
        one = y_copy(zz, 1 - y)
        one.start()
        started.append(one)

    def z_copy(zz, source_z, peer):
        return copy(
            core_buf.at[zz * 2 + y],
            z_buf.at[source_z],
            z_send.at[zz],
            z_recv.at[source_z],
            peer,
        )

    for step in (2, 1, 3, 0):
        zz = lax.rem(z + step, 4)
        add_core(zz, y)
        y_copy(zz, y).wait_recv()
        if step == 0:
            continue
        place = zz * 2 + y
        for start in range(0, columns, width):
            cut = pl.ds(start, width)
            total = core_buf[place, :, cut].astype(jnp.float32) + y_buf[zz, :, cut].astype(
                jnp.float32
            )
            core_buf[place, :, cut] = total.astype(core_buf.dtype)
        one = z_copy(zz, z, along_z[step - 1])
        one.start()
        started.append(one)
    for step in (1, 3, 2):
        zz = lax.rem(z + step, 4)
        z_copy(zz, zz, along_z[step - 1]).wait_recv()
    for start in range(0, columns, width):
        cut = pl.ds(start, width)
        total = core_buf[z * 2 + y, :, cut].astype(jnp.float32) + y_buf[z, :, cut].astype(
            jnp.float32
        )
        for step in (1, 2, 3):
            total = total + z_buf[lax.rem(z + step, 4), :, cut].astype(jnp.float32)
        out_ref[:, cut] = total
    for one in started:
        one.wait_send()


def scatter_mp(partial, collective_id):
    count = lax.axis_size("mp")
    tokens, columns = partial.shape
    rows = tokens // count
    dma = pltpu.SemaphoreType.DMA
    return pl.pallas_call(
        scatter_kernel,
        out_shape=jax.ShapeDtypeStruct((rows, columns), jnp.float32),
        in_specs=[pl.BlockSpec(memory_space=pltpu.VMEM)],
        out_specs=pl.BlockSpec(memory_space=pltpu.VMEM),
        scratch_shapes=[
            pltpu.VMEM((8, rows, columns), partial.dtype),
            pltpu.VMEM((4, rows, columns), partial.dtype),
            pltpu.VMEM((4, rows, columns), partial.dtype),
            dma((8,)),
            dma((8,)),
            dma((4,)),
            dma((4,)),
            dma((4,)),
            dma((4,)),
        ],
        compiler_params=pltpu.CompilerParams(
            collective_id=collective_id, has_side_effects=True, vmem_limit_bytes=40 * 2**20
        ),
        cost_estimate=pl.CostEstimate(flops=30 * 10**9, bytes_accessed=10**7, transcendentals=0),
    )(partial.reshape(count, rows, columns))


def project_kernel(tokens_ref, weight_ref, out_ref):
    out_ref[...] = jnp.dot(
        tokens_ref[...], weight_ref[...].astype(jnp.bfloat16), preferred_element_type=jnp.float32
    ).astype(out_ref.dtype)


def project(tokens, weight, dtype):
    count, depth = tokens.shape
    columns = weight.shape[1]
    width = 256
    return pl.pallas_call(
        project_kernel,
        grid=(columns // width,),
        out_shape=jax.ShapeDtypeStruct((count, columns), dtype),
        in_specs=[
            pl.BlockSpec((count, depth), lambda i: (0, 0)),
            pl.BlockSpec((depth, width), lambda i: (0, i)),
        ],
        out_specs=pl.BlockSpec((count, width), lambda i: (0, i)),
        compiler_params=pltpu.CompilerParams(vmem_limit_bytes=32 * 2**20),
        cost_estimate=pl.CostEstimate(
            flops=2 * count * depth * columns,
            bytes_accessed=4 * depth * columns + 2 * count * (depth + columns),
            transcendentals=0,
        ),
    )(tokens, weight)


def split_rows(block):
    half = block.shape[1] // 2
    index = lax.axis_index("dp")
    own = lax.dynamic_slice_in_dim(block, index * half, half, 1)
    other = lax.dynamic_slice_in_dim(block, (1 - index) * half, half, 1)
    return own, other


def on_device_pair(
    inputs,
    lengths,
    gain_in,
    query_weight,
    key_weight,
    value_weight,
    output_weight,
    gain_post,
    gain_pre,
    gate_weight,
    up_weight,
):
    bf16 = jnp.bfloat16
    slot = inputs.shape[0] * lax.axis_size("mp")
    length = lengths[0]
    normed_local = rms_norm(inputs.astype(jnp.float32), gain_in).astype(bf16)
    own_rows, other_rows = split_rows(normed_local)
    partner_tokens = gather_mp(other_rows, True, 0)
    qkv_weight = jnp.concatenate([query_weight, key_weight, value_weight], axis=1).astype(bf16)
    head_size = key_weight.shape[1]
    local_heads = query_weight.shape[1] // head_size
    partner_part = jnp.dot(partner_tokens, qkv_weight, preferred_element_type=jnp.float32)
    partner_part = partner_part.astype(bf16)
    own_rows = lax.optimization_barrier((partner_part, own_rows))[1]
    arrived = swap_dp(partner_part)
    own_tokens = gather_mp(own_rows, False, 1)
    raw = jnp.dot(own_tokens, qkv_weight, preferred_element_type=jnp.float32)
    raw = raw + arrived.astype(jnp.float32)
    q_cols = local_heads * head_size
    raw_q, raw_k, raw_v = (
        raw[:, :q_cols],
        raw[:, q_cols : q_cols + head_size],
        raw[:, q_cols + head_size :],
    )
    positions = jnp.arange(slot, dtype=jnp.int32)
    live = positions < length
    queries = rotate_pairs(raw_q.reshape(slot, local_heads, head_size), positions).astype(bf16)
    keys_rot = rotate_pairs(raw_k.reshape(slot, 1, head_size), positions).reshape(slot, head_size)
    keys_rot = jnp.where(live[:, None], keys_rot, jnp.float32(0.0)).astype(bf16)
    values_all = jnp.where(live[:, None], raw_v, jnp.float32(0.0)).astype(bf16)
    mixed = head_block(queries, keys_rot, values_all, slot, length)
    mixed = jnp.where(live[:, None, None], mixed, jnp.float32(0.0))
    attended = mixed.astype(bf16).reshape(slot, local_heads * head_size)
    attn_rows = scatter_mp(
        jnp.dot(attended, output_weight, preferred_element_type=jnp.float32).astype(bf16), 2
    )
    residual = (inputs.astype(jnp.float32) + rms_norm(attn_rows, gain_post)).astype(bf16)
    pre_local = rms_norm(residual.astype(jnp.float32), gain_pre).astype(bf16)
    own_rows, other_rows = split_rows(pre_local)
    partner_tokens = gather_mp(other_rows, True, 3)
    gate_part = project(partner_tokens, gate_weight, bf16)
    gate_sent = swap_dp(gate_part)
    up_tokens = lax.optimization_barrier((partner_tokens, gate_part))[0]
    up_part = project(up_tokens, up_weight, bf16)
    up_sent = swap_dp(up_part)
    own_rows = lax.optimization_barrier((own_rows, up_part))[0]
    own_tokens = gather_mp(own_rows, False, 4)
    gate = project(own_tokens, gate_weight, jnp.float32) + gate_sent.astype(jnp.float32)
    up = project(own_tokens, up_weight, jnp.float32) + up_sent.astype(jnp.float32)
    hidden = (jax.nn.gelu(gate, approximate=True) * up).astype(bf16)
    return (residual, hidden, keys_rot, values_all)


def solution(mesh):
    pair_form = mesh.shape["dp"] == 2 and mesh.shape["mp"] == KVH
    in_specs = (
        P(("dp", "mp"), None),
        P("dp"),
        P(),
        P("dp", "mp"),
        P("dp", "mp"),
        P("dp", "mp"),
        P("mp", None),
        P(),
        P(),
        P("dp", "mp"),
        P("dp", "mp"),
    )
    out_specs = (P(("dp", "mp"), None), P("dp", "mp"), P("dp", "mp"), P("dp", "mp"))
    return jax.shard_map(
        on_device_pair if pair_form else on_device, mesh=mesh, in_specs=in_specs, out_specs=out_specs, check_vma=False
    )
```
